32 devices in a mesh: clip: 4 (over y, core), ctx: 8 (over z, x).
Axes of the slice: x: 2, y: 2, z: 4, core: 2. Of those that a mesh axis runs over, the one named last changes fastest.
Arguments:
- queries: bfloat16 [4096, 4096], P(('clip', 'ctx')), parts along dimension 0, may hold values from -48 to 48
- key_rows: bfloat16 [4096, 4096], P(('clip', 'ctx')), parts along dimension 0, may hold values from -48 to 48
- values: bfloat16 [4096, 4096], P(('clip', 'ctx')), parts along dimension 0, may hold values from -6 to 6
- tangent_queries: bfloat16 [4096, 4096], P(('clip', 'ctx')), parts along dimension 0, may hold values from -6 to 6
- tangent_keys: bfloat16 [4096, 4096], P(('clip', 'ctx')), parts along dimension 0, may hold values from -6 to 6
- tangent_values: bfloat16 [4096, 4096], P(('clip', 'ctx')), parts along dimension 0, may hold values from -6 to 6
Outputs:
- attended: bfloat16 [4096, 4096], P(('clip', 'ctx')), parts along dimension 0
- tangent_output: bfloat16 [4096, 4096], P(('clip', 'ctx')), parts along dimension 0
The draws below stay inside these ranges and needn't reach their ends.
There are 4 independent parts, one for each index of `clip`. The reference program is written for one: setup_inputs(seed, part) draws one part's arguments, and reference() takes and returns one part's arrays. A program takes and returns all parts, laid end to end along the dimension named above; each array names one. Nothing has to cross between parts.
All inputs are finite; a program needn't handle non-finite values.
Results may differ from the reference program's by a relative error of at most 0.012.
Values may be sent and summed in bfloat16 or wider, within the bound.
A program may use at most 64 MiB of HBM per device.

```python
import jax
import jax.numpy as jnp
from jax import lax

HD = 128
HEADS = 32
TOKENS = 1024


def draw_queries(key, part):
    drawn = jnp.clip(jax.random.normal(jax.random.fold_in(key, 1), (TOKENS, HEADS * HD), jnp.float32), -6.0, 6.0)
    return drawn.astype(jnp.bfloat16)


def draw_key_rows(key, part):
    drawn = jnp.clip(jax.random.normal(jax.random.fold_in(key, 2), (TOKENS, HEADS * HD), jnp.float32), -6.0, 6.0)
    return drawn.astype(jnp.bfloat16)


def steps_of(stream_key, shape, cuts, low, high):
    def one(dim, parts):
        draws = jax.random.uniform(jax.random.fold_in(jax.random.fold_in(stream_key, 6), dim), (parts,), jnp.float32, low / len(cuts), high / len(cuts))
        return jnp.repeat(jnp.exp(draws), shape[dim] // parts).reshape((-1,) + (1,) * (len(shape) - dim - 1))

    level = one(*cuts[0])
    for cut in cuts[1:]:
        level = level * one(*cut)
    return level


def scatter_about(stream_key, extent, width, limit, pieces=(), held_as=jnp.bfloat16):
    factor_of = steps_of(stream_key, extent, pieces, -0.22, 0.18) if pieces else 1.0
    entries = jax.random.normal(stream_key, extent, jnp.float32) * width * factor_of
    return jnp.minimum(jnp.maximum(entries, -limit), limit).astype(held_as)


def setup_inputs(seed: int = 0, part: int = 0) -> dict:
    keys = jax.random.split(jax.random.key(seed), 7)
    own_keys = jax.random.split(jax.random.fold_in(keys[6], part), 7)
    queries = draw_queries(jax.random.fold_in(jax.random.fold_in(keys[6], part), 71), part)
    key_rows = draw_key_rows(jax.random.fold_in(jax.random.fold_in(keys[6], part), 71), part)
    values = scatter_about(own_keys[2], (TOKENS, HEADS * HD), 1.0, 6.0, ((0, 8),))
    tangent_queries = scatter_about(own_keys[3], (TOKENS, HEADS * HD), 1.0, 6.0, ((0, 8),))
    tangent_keys = scatter_about(own_keys[4], (TOKENS, HEADS * HD), 1.0, 6.0, ((0, 8),))
    tangent_values = scatter_about(own_keys[5], (TOKENS, HEADS * HD), 1.0, 6.0, ((0, 8),))
    return dict(queries=queries, key_rows=key_rows, values=values, tangent_queries=tangent_queries, tangent_keys=tangent_keys, tangent_values=tangent_values)


def reference(queries, key_rows, values, tangent_queries, tangent_keys, tangent_values):
    scale = HD ** -0.5

    def by_heads(array):
        return jnp.transpose(array.reshape(TOKENS, HEADS, HD), (1, 0, 2))

    def side_by_side(array):
        return jnp.transpose(array, (1, 0, 2)).reshape(TOKENS, HEADS * HD)

    def one_head(group):
        query_head, key_head, value_head, tquery_head, tkey_head, tvalue_head = group
        scores = jnp.dot(query_head, key_head.T, preferred_element_type=jnp.float32) * scale
        probs = jax.nn.softmax(scores, axis=-1)
        dscores = (jnp.dot(tquery_head, key_head.T, preferred_element_type=jnp.float32)
                   + jnp.dot(query_head, tkey_head.T, preferred_element_type=jnp.float32)) * scale
        weighted = probs * dscores
        correction = jnp.sum(weighted, axis=-1, keepdims=True)
        prob_half = probs.astype(jnp.bfloat16)
        weight_half = weighted.astype(jnp.bfloat16)
        primal = jnp.dot(prob_half, value_head, preferred_element_type=jnp.float32)
        tangent = (jnp.dot(weight_half, value_head, preferred_element_type=jnp.float32)
                   + jnp.dot(prob_half, tvalue_head, preferred_element_type=jnp.float32)
                   - correction * primal)
        return primal.astype(jnp.bfloat16), tangent.astype(jnp.bfloat16)

    results = lax.map(one_head, tuple(by_heads(array) for array in (queries, key_rows, values, tangent_queries, tangent_keys, tangent_values)))
    return (side_by_side(results[0]), side_by_side(results[1]))
```

```python
import functools

import jax
import jax.numpy as jnp
from jax import lax
from jax.experimental import pallas as pl
from jax.experimental.pallas import tpu as pltpu
from jax.sharding import PartitionSpec as P

HD = 128
ARRAYS = 6
PLACE = ((0, 1), (1, 0), (2, 0), (0, 0), (1, 1), (2, 1))


def across_first(me, step, count):
    if count % 2:
        return lax.rem(me + 1 + step, count)
    half = count // 2
    side = me // half
    other = lax.rem(step // half + 1 + side, 2)
    return other * half + lax.rem(me + step, half)


def alternating(me, step, count):
    if count % 2:
        return lax.rem(me + 1 + step, count)
    half = count // 2
    side = me // half
    other = lax.rem(step + 1 + side, 2)
    return other * half + lax.rem(me + step // 2, half)


def wait_bytes(ref, sem):
    pltpu.make_async_copy(ref, ref, sem).wait()


def kernel(n, heads, rows, per, *refs):
    inputs = refs[:ARRAYS]
    outs = refs[ARRAYS:ARRAYS + 2]
    big, res, send_sem, recv_sem, own_sem, osend_sem, orecv_sem, oown_sem = refs[ARRAYS + 2:]
    me = lax.axis_index("ctx")
    total = n * rows
    rest = total - rows
    block = per * rows
    blocks = n // per
    scale = HD ** (-0.5)

    barrier = pltpu.get_barrier_semaphore()

    @pl.loop(1, n)
    def _(step):
        pl.semaphore_signal(barrier, inc=1, device_id={"ctx": lax.rem(me + step, n)})

    def columns(device, h):
        return pl.ds(pl.multiple_of((device * heads + h) * HD, HD), HD)

    def token_rows(device):
        return pl.ds(pl.multiple_of(device * rows, rows), rows)

    def landing(a, h):
        pair, half = PLACE[a]
        return big.at[h, pair, token_rows(me), pl.ds(half * HD, HD)]

    def own_in(a, h):
        return pltpu.make_async_copy(inputs[a].at[:, columns(me, h)], landing(a, h), own_sem.at[h, a])

    @pl.loop(0, heads)
    def _(h):
        for a in range(ARRAYS):
            own_in(a, h).start()

    pl.semaphore_wait(barrier, n - 1)

    @pl.loop(0, heads)
    def _(h):
        @pl.loop(0, n)
        def _(step):
            peer = alternating(me, step, n)

            @pl.when(peer != me)
            def _():
                for a in range(ARRAYS):
                    pltpu.make_async_remote_copy(
                        src_ref=inputs[a].at[:, columns(peer, h)],
                        dst_ref=landing(a, h),
                        send_sem=send_sem.at[h],
                        recv_sem=recv_sem.at[h],
                        device_id={"ctx": peer},
                    ).start()

    def own_out(i, h):
        return pltpu.make_async_copy(
            res.at[h, i, token_rows(me)], outs[i].at[:, columns(me, h)], oown_sem.at[h, i]
        )

    @pl.loop(0, heads)
    def _(h):
        for a in range(ARRAYS):
            own_in(a, h).wait()
        wait_bytes(big.at[h, :, pl.ds(0, rest), :], recv_sem.at[h])

        @pl.loop(0, blocks)
        def _(step):
            at = across_first(me // per, step, blocks)
            mine = pl.ds(pl.multiple_of(at * block, block), block)
            queries = big[h, 0, mine, :]
            scores = lax.dot_general(
                queries[:, HD:], big[h, 1, :, :HD], (((1,), (1,)), ((), ())),
                preferred_element_type=jnp.float32,
            )
            top = jnp.max(scores, axis=-1, keepdims=True)
            raised = jnp.exp((scores - top) * scale)
            inverse = 1.0 / jnp.sum(raised, axis=-1, keepdims=True)
            raised_half = raised.astype(jnp.bfloat16)
            dscores = lax.dot_general(
                queries, big[h, 1], (((1,), (1,)), ((), ())),
                preferred_element_type=jnp.float32,
            )
            weighted = raised * dscores
            correction = jnp.sum(weighted, axis=-1, keepdims=True) * (inverse * scale)
            both = jnp.dot(raised_half, big[h, 2], preferred_element_type=jnp.float32) * inverse
            along = jnp.dot(
                weighted.astype(jnp.bfloat16), big[h, 2, :, :HD], preferred_element_type=jnp.float32
            ) * (inverse * scale)
            primal = both[:, :HD]
            res[h, 0, mine, :] = primal.astype(jnp.bfloat16)
            res[h, 1, mine, :] = (along + both[:, HD:] - correction * primal).astype(jnp.bfloat16)

            for k in range(per):
                peer = at * per + k

                @pl.when(peer != me)
                def _():
                    for i in range(2):
                        pltpu.make_async_remote_copy(
                            src_ref=res.at[h, i, token_rows(peer)],
                            dst_ref=outs[i].at[:, columns(me, h)],
                            send_sem=osend_sem.at[h],
                            recv_sem=orecv_sem,
                            device_id={"ctx": peer},
                        ).start()

                @pl.when(peer == me)
                def _():
                    for i in range(2):
                        own_out(i, h).start()

    @pl.loop(0, heads)
    def _(h):
        wait_bytes(big.at[h, :, pl.ds(0, rest), :], send_sem.at[h])
        wait_bytes(res.at[h, :, pl.ds(0, rest), :], osend_sem.at[h])
        for i in range(2):
            own_out(i, h).wait()

    wait_bytes(res.at[:, :, pl.ds(0, rest), :], orecv_sem)


def body(*arrays):
    n = lax.axis_size("ctx")
    rows, width = arrays[0].shape
    heads = width // (n * HD)
    total = n * rows
    per = 2 if n % 2 == 0 and total <= 2048 else 1
    shape = jax.ShapeDtypeStruct((rows, width), jnp.bfloat16)
    anywhere = pl.BlockSpec(memory_space=pl.ANY)
    return pl.pallas_call(
        functools.partial(kernel, n, heads, rows, per),
        out_shape=(shape, shape),
        in_specs=[anywhere] * ARRAYS,
        out_specs=(anywhere, anywhere),
        scratch_shapes=[
            pltpu.VMEM((heads, 3, total, 2 * HD), jnp.bfloat16),
            pltpu.VMEM((heads, 2, total, HD), jnp.bfloat16),
            pltpu.SemaphoreType.DMA((heads,)),
            pltpu.SemaphoreType.DMA((heads,)),
            pltpu.SemaphoreType.DMA((heads, ARRAYS)),
            pltpu.SemaphoreType.DMA((heads,)),
            pltpu.SemaphoreType.DMA,
            pltpu.SemaphoreType.DMA((heads, 2)),
        ],
        compiler_params=pltpu.CompilerParams(
            collective_id=0, has_side_effects=True, vmem_limit_bytes=50 * 2**20
        ),
        cost_estimate=pl.CostEstimate(
            flops=12 * heads * total * total * HD,
            bytes_accessed=2 * 8 * rows * width,
            transcendentals=heads * total * total,
        ),
    )(*arrays)


def solution(mesh):
    spec = P(("clip", "ctx"), None)
    return jax.shard_map(
        body, mesh=mesh, in_specs=(spec,) * ARRAYS, out_specs=(spec, spec), check_vma=False
    )
```

```python
import functools

import jax
import jax.numpy as jnp
from jax import lax
from jax.experimental import pallas as pl
from jax.experimental.pallas import tpu as pltpu
from jax.sharding import PartitionSpec as P

HD = 128
ARRAYS = 6
PLACE = ((0, 1), (1, 0), (2, 0), (0, 0), (1, 1), (2, 1))


def across_first(me, step, count):
    if count % 2:
        return lax.rem(me + 1 + step, count)
    half = count // 2
    side = me // half
    other = lax.rem(step // half + 1 + side, 2)
    return other * half + lax.rem(me + step, half)


def alternating(me, step, count):
    if count % 2:
        return lax.rem(me + 1 + step, count)
    half = count // 2
    side = me // half
    other = lax.rem(step + 1 + side, 2)
    return other * half + lax.rem(me + step // 2, half)


def wait_bytes(ref, sem):
    pltpu.make_async_copy(ref, ref, sem).wait()


def kernel(n, heads, rows, per, *refs):
    inputs = refs[:ARRAYS]
    outs = refs[ARRAYS:ARRAYS + 2]
    big, res, send_sem, recv_sem, own_sem, osend_sem, orecv_sem, oown_sem = refs[ARRAYS + 2:]
    me = lax.axis_index("ctx")
    total = n * rows
    rest = total - rows
    block = per * rows
    blocks = n // per
    scale = HD ** (-0.5)

    barrier = pltpu.get_barrier_semaphore()

    @pl.loop(1, n)
    def _(step):
        pl.semaphore_signal(barrier, inc=1, device_id={"ctx": lax.rem(me + step, n)})

    def columns(device, h):
        return pl.ds(pl.multiple_of((device * heads + h) * HD, HD), HD)

    def token_rows(device):
        return pl.ds(pl.multiple_of(device * rows, rows), rows)

    def landing(a, h):
        pair, half = PLACE[a]
        return big.at[h, pair, token_rows(me), pl.ds(half * HD, HD)]

    def own_in(a, h):
        return pltpu.make_async_copy(inputs[a].at[:, columns(me, h)], landing(a, h), own_sem.at[h, a])

    @pl.loop(0, heads)
    def _(h):
        for a in range(ARRAYS):
            own_in(a, h).start()

    pl.semaphore_wait(barrier, n - 1)

    @pl.loop(0, heads)
    def _(h):
        @pl.loop(0, n)
        def _(step):
            peer = alternating(me, step, n)

            @pl.when(peer != me)
            def _():
                for a in range(ARRAYS):
                    pltpu.make_async_remote_copy(
                        src_ref=inputs[a].at[:, columns(peer, h)],
                        dst_ref=landing(a, h),
                        send_sem=send_sem.at[h],
                        recv_sem=recv_sem.at[h],
                        device_id={"ctx": peer},
                    ).start()

    def own_out(i, h):
        return pltpu.make_async_copy(
            res.at[h, i, token_rows(me)], outs[i].at[:, columns(me, h)], oown_sem.at[h, i]
        )

    def send_out(peer, h):
        @pl.when(peer != me)
        def _():
            for i in range(2):
                pltpu.make_async_remote_copy(
                    src_ref=res.at[h, i, token_rows(peer)],
                    dst_ref=outs[i].at[:, columns(me, h)],
                    send_sem=osend_sem.at[h],
                    recv_sem=orecv_sem,
                    device_id={"ctx": peer},
                ).start()

        @pl.when(peer == me)
        def _():
            for i in range(2):
                own_out(i, h).start()

    def send_head(h):
        @pl.loop(0, n)
        def _(step):
            send_out(alternating(me, step, n), h)

    @pl.loop(0, heads)
    def _(h):
        for a in range(ARRAYS):
            own_in(a, h).wait()
        wait_bytes(big.at[h, :, pl.ds(0, rest), :], recv_sem.at[h])

        @pl.when(h == heads - 1)
        def _():
            @pl.loop(1 if heads > 2 else 0, heads - 1)
            def _(early):
                send_head(early)

        @pl.loop(0, blocks)
        def _(step):
            at = across_first(me // per, step, blocks)
            mine = pl.ds(pl.multiple_of(at * block, block), block)
            queries = big[h, 0, mine, :]
            scores = lax.dot_general(
                queries[:, HD:], big[h, 1, :, :HD], (((1,), (1,)), ((), ())),
                preferred_element_type=jnp.float32,
            )
            top = jnp.max(scores, axis=-1, keepdims=True)
            raised = jnp.exp((scores - top) * scale)
            inverse = 1.0 / jnp.sum(raised, axis=-1, keepdims=True)
            raised_half = raised.astype(jnp.bfloat16)
            dscores = lax.dot_general(
                queries, big[h, 1], (((1,), (1,)), ((), ())),
                preferred_element_type=jnp.float32,
            )
            weighted = raised * dscores
            correction = jnp.sum(weighted, axis=-1, keepdims=True) * (inverse * scale)
            both = jnp.dot(raised_half, big[h, 2], preferred_element_type=jnp.float32) * inverse
            along = jnp.dot(
                weighted.astype(jnp.bfloat16), big[h, 2, :, :HD], preferred_element_type=jnp.float32
            ) * (inverse * scale)
            primal = both[:, :HD]
            res[h, 0, mine, :] = primal.astype(jnp.bfloat16)
            res[h, 1, mine, :] = (along + both[:, HD:] - correction * primal).astype(jnp.bfloat16)

            @pl.when(h == heads - 1)
            def _():
                for k in range(per):
                    send_out(at * per + k, h)

        @pl.when((h == heads - 2) & (heads > 2))
        def _():
            send_head(0)

    @pl.loop(0, heads)
    def _(h):
        wait_bytes(big.at[h, :, pl.ds(0, rest), :], send_sem.at[h])
        wait_bytes(res.at[h, :, pl.ds(0, rest), :], osend_sem.at[h])
        for i in range(2):
            own_out(i, h).wait()

    wait_bytes(res.at[:, :, pl.ds(0, rest), :], orecv_sem)


def body(*arrays):
    n = lax.axis_size("ctx")
    rows, width = arrays[0].shape
    heads = width // (n * HD)
    total = n * rows
    per = 2 if n % 2 == 0 and total <= 2048 else 1
    shape = jax.ShapeDtypeStruct((rows, width), jnp.bfloat16)
    anywhere = pl.BlockSpec(memory_space=pl.ANY)
    in_hbm = pl.BlockSpec(memory_space=pltpu.HBM)
    return pl.pallas_call(
        functools.partial(kernel, n, heads, rows, per),
        out_shape=(shape, shape),
        in_specs=[in_hbm] * ARRAYS,
        out_specs=(anywhere, anywhere),
        scratch_shapes=[
            pltpu.VMEM((heads, 3, total, 2 * HD), jnp.bfloat16),
            pltpu.VMEM((heads, 2, total, HD), jnp.bfloat16),
            pltpu.SemaphoreType.DMA((heads,)),
            pltpu.SemaphoreType.DMA((heads,)),
            pltpu.SemaphoreType.DMA((heads, ARRAYS)),
            pltpu.SemaphoreType.DMA((heads,)),
            pltpu.SemaphoreType.DMA,
            pltpu.SemaphoreType.DMA((heads, 2)),
        ],
        compiler_params=pltpu.CompilerParams(
            collective_id=0, has_side_effects=True, vmem_limit_bytes=50 * 2**20
        ),
        cost_estimate=pl.CostEstimate(
            flops=12 * heads * total * total * HD,
            bytes_accessed=2 * 8 * rows * width,
            transcendentals=heads * total * total,
        ),
    )(*arrays)


def solution(mesh):
    spec = P(("clip", "ctx"), None)
    return jax.shard_map(
        body, mesh=mesh, in_specs=(spec,) * ARRAYS, out_specs=(spec, spec), check_vma=False
    )
```

```python
import functools

import jax
import jax.numpy as jnp
from jax import lax
from jax.experimental import pallas as pl
from jax.experimental.pallas import tpu as pltpu
from jax.sharding import PartitionSpec as P

HD = 128
ARRAYS = 6
PLACE = ((0, 1), (1, 0), (2, 0), (0, 0), (1, 1), (2, 1))


def across_first(me, step, count):
    if count % 2:
        return lax.rem(me + 1 + step, count)
    half = count // 2
    side = me // half
    other = lax.rem(step // half + 1 + side, 2)
    return other * half + lax.rem(me + step, half)


def alternating(me, step, count):
    if count % 2:
        return lax.rem(me + 1 + step, count)
    half = count // 2
    side = me // half
    other = lax.rem(step + 1 + side, 2)
    return other * half + lax.rem(me + step // 2, half)


def wait_bytes(ref, sem):
    pltpu.make_async_copy(ref, ref, sem).wait()


def kernel(n, heads, rows, per, *refs):
    inputs = refs[:ARRAYS]
    outs = refs[ARRAYS:ARRAYS + 2]
    big, res, send_sem, recv_sem, own_sem, osend_sem, orecv_sem, oown_sem = refs[ARRAYS + 2:]
    me = lax.axis_index("ctx")
    total = n * rows
    rest = total - rows
    block = per * rows
    blocks = n // per
    scale = HD ** (-0.5)

    barrier = pltpu.get_barrier_semaphore()

    @pl.loop(1, n)
    def _(step):
        pl.semaphore_signal(barrier, inc=1, device_id={"ctx": lax.rem(me + step, n)})

    def columns(device, h):
        return pl.ds(pl.multiple_of((device * heads + h) * HD, HD), HD)

    def token_rows(device):
        return pl.ds(pl.multiple_of(device * rows, rows), rows)

    def landing(a, h):
        pair, half = PLACE[a]
        return big.at[h, pair, token_rows(me), pl.ds(half * HD, HD)]

    def own_in(a, h):
        return pltpu.make_async_copy(inputs[a].at[:, columns(me, h)], landing(a, h), own_sem.at[h, a])

    @pl.loop(0, heads)
    def _(h):
        for a in range(ARRAYS):
            own_in(a, h).start()

    pl.semaphore_wait(barrier, n - 1)

    def send_in(a, peer, h):
        pltpu.make_async_remote_copy(
            src_ref=inputs[a].at[:, columns(peer, h)],
            dst_ref=landing(a, h),
            send_sem=send_sem.at[h],
            recv_sem=recv_sem.at[h],
            device_id={"ctx": peer},
        ).start()

    turns = 2 if n % 2 == 0 else 1

    @pl.loop(0, heads)
    def _(h):
        @pl.loop(0, n // turns)
        def _(step):
            for a in range(ARRAYS):
                for turn in range(turns):
                    peer = alternating(me, step * turns + turn, n)

                    @pl.when(peer != me)
                    def _():
                        send_in(a, peer, h)

    def own_out(i, h):
        return pltpu.make_async_copy(
            res.at[h, i, token_rows(me)], outs[i].at[:, columns(me, h)], oown_sem.at[h, i]
        )

    @pl.loop(0, heads)
    def _(h):
        for a in range(ARRAYS):
            own_in(a, h).wait()
        wait_bytes(big.at[h, :, pl.ds(0, rest), :], recv_sem.at[h])

        @pl.loop(0, blocks)
        def _(step):
            at = across_first(me // per, step, blocks)
            mine = pl.ds(pl.multiple_of(at * block, block), block)
            queries = big[h, 0, mine, :]
            scores = lax.dot_general(
                queries[:, HD:], big[h, 1, :, :HD], (((1,), (1,)), ((), ())),
                preferred_element_type=jnp.float32,
            )
            top = jnp.max(scores, axis=-1, keepdims=True)
            raised = jnp.exp((scores - top) * scale)
            inverse = 1.0 / jnp.sum(raised, axis=-1, keepdims=True)
            raised_half = raised.astype(jnp.bfloat16)
            dscores = lax.dot_general(
                queries, big[h, 1], (((1,), (1,)), ((), ())),
                preferred_element_type=jnp.float32,
            )
            weighted = raised * dscores
            correction = jnp.sum(weighted, axis=-1, keepdims=True) * (inverse * scale)
            both = jnp.dot(raised_half, big[h, 2], preferred_element_type=jnp.float32) * inverse
            along = jnp.dot(
                weighted.astype(jnp.bfloat16), big[h, 2, :, :HD], preferred_element_type=jnp.float32
            ) * (inverse * scale)
            primal = both[:, :HD]
            res[h, 0, mine, :] = primal.astype(jnp.bfloat16)
            res[h, 1, mine, :] = (along + both[:, HD:] - correction * primal).astype(jnp.bfloat16)

            for k in range(per):
                peer = at * per + k

                @pl.when(peer != me)
                def _():
                    for i in range(2):
                        pltpu.make_async_remote_copy(
                            src_ref=res.at[h, i, token_rows(peer)],
                            dst_ref=outs[i].at[:, columns(me, h)],
                            send_sem=osend_sem.at[h],
                            recv_sem=orecv_sem,
                            device_id={"ctx": peer},
                        ).start()

                @pl.when(peer == me)
                def _():
                    for i in range(2):
                        own_out(i, h).start()

    @pl.loop(0, heads)
    def _(h):
        wait_bytes(big.at[h, :, pl.ds(0, rest), :], send_sem.at[h])
        wait_bytes(res.at[h, :, pl.ds(0, rest), :], osend_sem.at[h])
        for i in range(2):
            own_out(i, h).wait()

    wait_bytes(res.at[:, :, pl.ds(0, rest), :], orecv_sem)


def body(*arrays):
    n = lax.axis_size("ctx")
    rows, width = arrays[0].shape
    heads = width // (n * HD)
    total = n * rows
    per = 2 if n % 2 == 0 and total <= 2048 else 1
    shape = jax.ShapeDtypeStruct((rows, width), jnp.bfloat16)
    anywhere = pl.BlockSpec(memory_space=pl.ANY)
    return pl.pallas_call(
        functools.partial(kernel, n, heads, rows, per),
        out_shape=(shape, shape),
        in_specs=[anywhere] * ARRAYS,
        out_specs=(anywhere, anywhere),
        scratch_shapes=[
            pltpu.VMEM((heads, 3, total, 2 * HD), jnp.bfloat16),
            pltpu.VMEM((heads, 2, total, HD), jnp.bfloat16),
            pltpu.SemaphoreType.DMA((heads,)),
            pltpu.SemaphoreType.DMA((heads,)),
            pltpu.SemaphoreType.DMA((heads, ARRAYS)),
            pltpu.SemaphoreType.DMA((heads,)),
            pltpu.SemaphoreType.DMA,
            pltpu.SemaphoreType.DMA((heads, 2)),
        ],
        compiler_params=pltpu.CompilerParams(
            collective_id=0, has_side_effects=True, vmem_limit_bytes=50 * 2**20
        ),
        cost_estimate=pl.CostEstimate(
            flops=12 * heads * total * total * HD,
            bytes_accessed=2 * 8 * rows * width,
            transcendentals=heads * total * total,
        ),
    )(*arrays)


def solution(mesh):
    spec = P(("clip", "ctx"), None)
    return jax.shard_map(
        body, mesh=mesh, in_specs=(spec,) * ARRAYS, out_specs=(spec, spec), check_vma=False
    )
```

```python
import functools

import jax
import jax.numpy as jnp
from jax import lax
from jax.experimental import pallas as pl
from jax.experimental.pallas import tpu as pltpu
from jax.sharding import PartitionSpec as P

HD = 128
ARRAYS = 6
PLACE = ((0, 1), (1, 0), (2, 0), (0, 0), (1, 1), (2, 1))


def across_first(me, step, count):
    if count % 2:
        return lax.rem(me + 1 + step, count)
    half = count // 2
    side = me // half
    other = lax.rem(step // half + 1 + side, 2)
    return other * half + lax.rem(me + step, half)


def alternating(me, step, count):
    if count % 2:
        return lax.rem(me + 1 + step, count)
    half = count // 2
    side = me // half
    other = lax.rem(step + 1 + side, 2)
    return other * half + lax.rem(me + step // 2, half)


def wait_bytes(ref, sem):
    pltpu.make_async_copy(ref, ref, sem).wait()


def kernel(n, heads, rows, per, *refs):
    inputs = refs[:ARRAYS]
    outs = refs[ARRAYS:ARRAYS + 2]
    big, res, send_sem, recv_sem, own_sem, osend_sem, orecv_sem, oown_sem = refs[ARRAYS + 2:]
    me = lax.axis_index("ctx")
    total = n * rows
    rest = total - rows
    block = per * rows
    blocks = n // per
    scale = HD ** (-0.5)

    barrier = pltpu.get_barrier_semaphore()

    @pl.loop(1, n)
    def _(step):
        pl.semaphore_signal(barrier, inc=1, device_id={"ctx": lax.rem(me + step, n)})

    def columns(device, h):
        return pl.ds(pl.multiple_of((device * heads + h) * HD, HD), HD)

    def token_rows(device):
        return pl.ds(pl.multiple_of(device * rows, rows), rows)

    def landing(a, h):
        pair, half = PLACE[a]
        return big.at[h, pair, token_rows(me), pl.ds(half * HD, HD)]

    def own_in(a, h):
        return pltpu.make_async_copy(inputs[a].at[:, columns(me, h)], landing(a, h), own_sem.at[h, a])

    @pl.loop(0, heads)
    def _(h):
        for a in range(ARRAYS):
            own_in(a, h).start(priority=1)

    pl.semaphore_wait(barrier, n - 1)

    def send_in(a, peer, h):
        pltpu.make_async_remote_copy(
            src_ref=inputs[a].at[:, columns(peer, h)],
            dst_ref=landing(a, h),
            send_sem=send_sem.at[h],
            recv_sem=recv_sem.at[h],
            device_id={"ctx": peer},
        ).start()

    turns = 2 if n % 2 == 0 else 1

    @pl.loop(0, heads)
    def _(h):
        @pl.loop(0, n // turns)
        def _(step):
            for a in range(ARRAYS):
                for turn in range(turns):
                    peer = alternating(me, step * turns + turn, n)

                    @pl.when(peer != me)
                    def _():
                        send_in(a, peer, h)

    def own_out(i, h):
        return pltpu.make_async_copy(
            res.at[h, i, token_rows(me)], outs[i].at[:, columns(me, h)], oown_sem.at[h, i]
        )

    @pl.loop(0, heads)
    def _(h):
        for a in range(ARRAYS):
            own_in(a, h).wait()
        wait_bytes(big.at[h, :, pl.ds(0, rest), :], recv_sem.at[h])

        @pl.loop(0, blocks)
        def _(step):
            group = me // per
            at = jnp.where(
                h == heads - 1,
                across_first(group, step, blocks),
                alternating(group, step, blocks),
            )
            mine = pl.ds(pl.multiple_of(at * block, block), block)
            queries = big[h, 0, mine, :]
            scores = lax.dot_general(
                queries[:, HD:], big[h, 1, :, :HD], (((1,), (1,)), ((), ())),
                preferred_element_type=jnp.float32,
            )
            top = jnp.max(scores, axis=-1, keepdims=True)
            raised = jnp.exp((scores - top) * scale)
            inverse = 1.0 / jnp.sum(raised, axis=-1, keepdims=True)
            raised_half = raised.astype(jnp.bfloat16)
            dscores = lax.dot_general(
                queries, big[h, 1], (((1,), (1,)), ((), ())),
                preferred_element_type=jnp.float32,
            )
            weighted = raised * dscores
            correction = jnp.sum(weighted, axis=-1, keepdims=True) * (inverse * scale)
            both = jnp.dot(raised_half, big[h, 2], preferred_element_type=jnp.float32) * inverse
            along = jnp.dot(
                weighted.astype(jnp.bfloat16), big[h, 2, :, :HD], preferred_element_type=jnp.float32
            ) * (inverse * scale)
            primal = both[:, :HD]
            res[h, 0, mine, :] = primal.astype(jnp.bfloat16)
            res[h, 1, mine, :] = (along + both[:, HD:] - correction * primal).astype(jnp.bfloat16)

            for k in range(per):
                peer = at * per + k

                @pl.when(peer != me)
                def _():
                    for i in range(2):
                        pltpu.make_async_remote_copy(
                            src_ref=res.at[h, i, token_rows(peer)],
                            dst_ref=outs[i].at[:, columns(me, h)],
                            send_sem=osend_sem.at[h],
                            recv_sem=orecv_sem,
                            device_id={"ctx": peer},
                        ).start()

                @pl.when(peer == me)
                def _():
                    for i in range(2):
                        own_out(i, h).start(priority=1)

    @pl.loop(0, heads)
    def _(h):
        wait_bytes(big.at[h, :, pl.ds(0, rest), :], send_sem.at[h])
        wait_bytes(res.at[h, :, pl.ds(0, rest), :], osend_sem.at[h])
        for i in range(2):
            own_out(i, h).wait()

    wait_bytes(res.at[:, :, pl.ds(0, rest), :], orecv_sem)


def body(*arrays):
    n = lax.axis_size("ctx")
    rows, width = arrays[0].shape
    heads = width // (n * HD)
    total = n * rows
    per = 2 if n % 2 == 0 and total <= 2048 else 1
    shape = jax.ShapeDtypeStruct((rows, width), jnp.bfloat16)
    anywhere = pl.BlockSpec(memory_space=pl.ANY)
    return pl.pallas_call(
        functools.partial(kernel, n, heads, rows, per),
        out_shape=(shape, shape),
        in_specs=[anywhere] * ARRAYS,
        out_specs=(anywhere, anywhere),
        scratch_shapes=[
            pltpu.VMEM((heads, 3, total, 2 * HD), jnp.bfloat16),
            pltpu.VMEM((heads, 2, total, HD), jnp.bfloat16),
            pltpu.SemaphoreType.DMA((heads,)),
            pltpu.SemaphoreType.DMA((heads,)),
            pltpu.SemaphoreType.DMA((heads, ARRAYS)),
            pltpu.SemaphoreType.DMA((heads,)),
            pltpu.SemaphoreType.DMA,
            pltpu.SemaphoreType.DMA((heads, 2)),
        ],
        compiler_params=pltpu.CompilerParams(
            collective_id=0, has_side_effects=True, vmem_limit_bytes=51 * 2**20
        ),
        cost_estimate=pl.CostEstimate(
            flops=12 * heads * total * total * HD,
            bytes_accessed=2 * 8 * rows * width,
            transcendentals=heads * total * total,
        ),
    )(*arrays)


def solution(mesh):
    spec = P(("clip", "ctx"), None)
    return jax.shard_map(
        body, mesh=mesh, in_specs=(spec,) * ARRAYS, out_specs=(spec, spec), check_vma=False
    )
```

```python
import functools

import jax
import jax.numpy as jnp
from jax import lax
from jax.experimental import pallas as pl
from jax.experimental.pallas import tpu as pltpu
from jax.sharding import PartitionSpec as P

HD = 128
ARRAYS = 6


def across_first(me, step, count):
    if count % 2:
        return lax.rem(me + 1 + step, count)
    half = count // 2
    side = me // half
    other = lax.rem(step // half + 1 + side, 2)
    return other * half + lax.rem(me + step, half)


def alternating(me, step, count):
    if count % 2:
        return lax.rem(me + 1 + step, count)
    half = count // 2
    side = me // half
    other = lax.rem(step + 1 + side, 2)
    return other * half + lax.rem(me + step // 2, half)


def wait_bytes(ref, sem):
    pltpu.make_async_copy(ref, ref, sem).wait()


def kernel(n, heads, rows, per, *refs):
    inputs = refs[:ARRAYS]
    outs = refs[ARRAYS:ARRAYS + 2]
    big, res, send_sem, recv_sem, own_sem, osend_sem, orecv_sem, oown_sem = refs[ARRAYS + 2:]
    me = lax.axis_index("ctx")
    total = n * rows
    rest = total - rows
    block = per * rows
    blocks = n // per
    scale = HD ** (-0.5)

    barrier = pltpu.get_barrier_semaphore()

    @pl.loop(1, n)
    def _(step):
        pl.semaphore_signal(barrier, inc=1, device_id={"ctx": lax.rem(me + step, n)})

    def columns(device, h):
        return pl.ds(pl.multiple_of((device * heads + h) * HD, HD), HD)

    def token_rows(device):
        return pl.ds(pl.multiple_of(device * rows, rows), rows)

    def landing(a, h):
        return big.at[h, a, token_rows(me), :]

    def own_in(a, h):
        return pltpu.make_async_copy(inputs[a].at[:, columns(me, h)], landing(a, h), own_sem.at[h, a])

    @pl.loop(0, heads)
    def _(h):
        for a in range(ARRAYS):
            own_in(a, h).start(priority=1)

    pl.semaphore_wait(barrier, n - 1)

    def send_in(a, peer, h):
        pltpu.make_async_remote_copy(
            src_ref=inputs[a].at[:, columns(peer, h)],
            dst_ref=landing(a, h),
            send_sem=send_sem.at[h],
            recv_sem=recv_sem.at[h],
            device_id={"ctx": peer},
        ).start()

    turns = 2 if n % 2 == 0 else 1

    @pl.loop(0, heads)
    def _(h):
        @pl.loop(0, n // turns)
        def _(step):
            for a in range(ARRAYS):
                for turn in range(turns):
                    peer = alternating(me, step * turns + turn, n)

                    @pl.when(peer != me)
                    def _():
                        send_in(a, peer, h)

    def own_out(i, h):
        return pltpu.make_async_copy(
            res.at[h, i, token_rows(me)], outs[i].at[:, columns(me, h)], oown_sem.at[h, i]
        )

    @pl.loop(0, heads)
    def _(h):
        for a in range(ARRAYS):
            own_in(a, h).wait()
        wait_bytes(big.at[h, :, pl.ds(0, rest), :], recv_sem.at[h])

        @pl.loop(0, blocks)
        def _(step):
            group = me // per
            at = jnp.where(
                h == heads - 1,
                across_first(group, step, blocks),
                alternating(group, step, blocks),
            )
            mine = pl.ds(pl.multiple_of(at * block, block), block)
            queries = big[h, 0, mine, :]
            both_queries = jnp.concatenate([big[h, 3, mine, :], queries], axis=-1)
            scores = lax.dot_general(
                queries, big[h, 1], (((1,), (1,)), ((), ())),
                preferred_element_type=jnp.float32,
            )
            top = jnp.max(scores, axis=-1, keepdims=True)
            raised = jnp.exp((scores - top) * scale)
            inverse = 1.0 / jnp.sum(raised, axis=-1, keepdims=True)
            raised_half = raised.astype(jnp.bfloat16)
            dscores = lax.dot_general(
                both_queries, jnp.concatenate([big[h, 1], big[h, 4]], axis=-1),
                (((1,), (1,)), ((), ())), preferred_element_type=jnp.float32,
            )
            weighted = raised * dscores
            correction = jnp.sum(weighted, axis=-1, keepdims=True) * (inverse * scale)
            both = jnp.dot(
                raised_half, jnp.concatenate([big[h, 2], big[h, 5]], axis=-1),
                preferred_element_type=jnp.float32,
            ) * inverse
            along = jnp.dot(
                weighted.astype(jnp.bfloat16), big[h, 2], preferred_element_type=jnp.float32
            ) * (inverse * scale)
            primal = both[:, :HD]
            res[h, 0, mine, :] = primal.astype(jnp.bfloat16)
            res[h, 1, mine, :] = (along + both[:, HD:] - correction * primal).astype(jnp.bfloat16)

            for k in range(per):
                peer = at * per + k

                @pl.when(peer != me)
                def _():
                    for i in range(2):
                        pltpu.make_async_remote_copy(
                            src_ref=res.at[h, i, token_rows(peer)],
                            dst_ref=outs[i].at[:, columns(me, h)],
                            send_sem=osend_sem.at[h],
                            recv_sem=orecv_sem,
                            device_id={"ctx": peer},
                        ).start()

                @pl.when(peer == me)
                def _():
                    for i in range(2):
                        own_out(i, h).start(priority=1)

    @pl.loop(0, heads)
    def _(h):
        wait_bytes(big.at[h, :, pl.ds(0, rest), :], send_sem.at[h])
        wait_bytes(res.at[h, :, pl.ds(0, rest), :], osend_sem.at[h])
        for i in range(2):
            own_out(i, h).wait()

    wait_bytes(res.at[:, :, pl.ds(0, rest), :], orecv_sem)


def body(*arrays):
    n = lax.axis_size("ctx")
    rows, width = arrays[0].shape
    heads = width // (n * HD)
    total = n * rows
    per = 2 if n % 2 == 0 and total <= 2048 else 1
    shape = jax.ShapeDtypeStruct((rows, width), jnp.bfloat16)
    anywhere = pl.BlockSpec(memory_space=pl.ANY)
    return pl.pallas_call(
        functools.partial(kernel, n, heads, rows, per),
        out_shape=(shape, shape),
        in_specs=[anywhere] * ARRAYS,
        out_specs=(anywhere, anywhere),
        scratch_shapes=[
            pltpu.VMEM((heads, ARRAYS, total, HD), jnp.bfloat16),
            pltpu.VMEM((heads, 2, total, HD), jnp.bfloat16),
            pltpu.SemaphoreType.DMA((heads,)),
            pltpu.SemaphoreType.DMA((heads,)),
            pltpu.SemaphoreType.DMA((heads, ARRAYS)),
            pltpu.SemaphoreType.DMA((heads,)),
            pltpu.SemaphoreType.DMA,
            pltpu.SemaphoreType.DMA((heads, 2)),
        ],
        compiler_params=pltpu.CompilerParams(
            collective_id=0, has_side_effects=True, vmem_limit_bytes=51 * 2**20
        ),
        cost_estimate=pl.CostEstimate(
            flops=12 * heads * total * total * HD,
            bytes_accessed=2 * 8 * rows * width,
            transcendentals=heads * total * total,
        ),
    )(*arrays)


def solution(mesh):
    spec = P(("clip", "ctx"), None)
    return jax.shard_map(
        body, mesh=mesh, in_specs=(spec,) * ARRAYS, out_specs=(spec, spec), check_vma=False
    )
```

```python
import functools

import jax
import jax.numpy as jnp
from jax import lax
from jax.experimental import pallas as pl
from jax.experimental.pallas import tpu as pltpu
from jax.sharding import PartitionSpec as P

HD = 128
ARRAYS = 6
PLACE = ((0, 1), (1, 0), (2, 0), (0, 0), (1, 1), (2, 1))


def across_first(me, step, count):
    if count % 2:
        return lax.rem(me + 1 + step, count)
    half = count // 2
    side = me // half
    other = lax.rem(step // half + 1 + side, 2)
    return other * half + lax.rem(me + step, half)


def alternating(me, step, count):
    if count % 2:
        return lax.rem(me + 1 + step, count)
    half = count // 2
    side = me // half
    other = lax.rem(step + 1 + side, 2)
    return other * half + lax.rem(me + step // 2, half)


def wait_bytes(ref, sem):
    pltpu.make_async_copy(ref, ref, sem).wait()


def kernel(n, heads, rows, per, *refs):
    inputs = refs[:ARRAYS]
    outs = refs[ARRAYS:ARRAYS + 2]
    big, res, send_sem, recv_sem, own_sem, osend_sem, orecv_sem, oown_sem = refs[ARRAYS + 2:]
    me = lax.axis_index("ctx")
    total = n * rows
    rest = total - rows
    block = per * rows
    blocks = n // per
    scale = HD ** (-0.5)

    barrier = pltpu.get_barrier_semaphore()

    @pl.loop(1, n)
    def _(step):
        pl.semaphore_signal(barrier, inc=1, device_id={"ctx": lax.rem(me + step, n)})

    def columns(device, h):
        return pl.ds(pl.multiple_of((device * heads + h) * HD, HD), HD)

    def token_rows(device):
        return pl.ds(pl.multiple_of(device * rows, rows), rows)

    def landing(a, h):
        pair, half = PLACE[a]
        return big.at[h, pair, token_rows(me), pl.ds(half * HD, HD)]

    def own_in(a, h):
        return pltpu.make_async_copy(inputs[a].at[:, columns(me, h)], landing(a, h), own_sem.at[h, a])

    @pl.loop(0, heads)
    def _(h):
        for a in range(ARRAYS):
            own_in(a, h).start(priority=1)

    pl.semaphore_wait(barrier, n - 1)

    def send_in(a, peer, h):
        pltpu.make_async_remote_copy(
            src_ref=inputs[a].at[:, columns(peer, h)],
            dst_ref=landing(a, h),
            send_sem=send_sem.at[h],
            recv_sem=recv_sem.at[h],
            device_id={"ctx": peer},
        ).start()

    turns = 2 if n % 2 == 0 else 1

    @pl.loop(0, heads)
    def _(h):
        @pl.loop(0, n // turns)
        def _(step):
            for a in range(ARRAYS):
                for turn in range(turns):
                    peer = alternating(me, step * turns + turn, n)

                    @pl.when(peer != me)
                    def _():
                        send_in(a, peer, h)

    def own_out(i, h):
        return pltpu.make_async_copy(
            res.at[h, i, token_rows(me)], outs[i].at[:, columns(me, h)], oown_sem.at[h, i]
        )

    def send_out(i, peer, h):
        @pl.when(peer != me)
        def _():
            pltpu.make_async_remote_copy(
                src_ref=res.at[h, i, token_rows(peer)],
                dst_ref=outs[i].at[:, columns(me, h)],
                send_sem=osend_sem.at[h],
                recv_sem=orecv_sem,
                device_id={"ctx": peer},
            ).start()

        @pl.when(peer == me)
        def _():
            own_out(i, h).start(priority=1)

    @pl.loop(0, heads)
    def _(h):
        for a in range(ARRAYS):
            own_in(a, h).wait()
        wait_bytes(big.at[h, :, pl.ds(0, rest), :], recv_sem.at[h])

        @pl.loop(0, blocks)
        def _(step):
            group = me // per
            at = jnp.where(
                h == heads - 1,
                across_first(group, step, blocks),
                alternating(group, step, blocks),
            )
            mine = pl.ds(pl.multiple_of(at * block, block), block)
            queries = big[h, 0, mine, :]
            scores = lax.dot_general(
                queries[:, HD:], big[h, 1, :, :HD], (((1,), (1,)), ((), ())),
                preferred_element_type=jnp.float32,
            )
            top = jnp.max(scores, axis=-1, keepdims=True)
            raised = jnp.exp((scores - top) * scale)
            inverse = 1.0 / jnp.sum(raised, axis=-1, keepdims=True)
            raised_half = raised.astype(jnp.bfloat16)
            dscores = lax.dot_general(
                queries, big[h, 1], (((1,), (1,)), ((), ())),
                preferred_element_type=jnp.float32,
            )
            weighted = raised * dscores
            correction = jnp.sum(weighted, axis=-1, keepdims=True) * (inverse * scale)
            both = jnp.dot(raised_half, big[h, 2], preferred_element_type=jnp.float32) * inverse
            along = jnp.dot(
                weighted.astype(jnp.bfloat16), big[h, 2, :, :HD], preferred_element_type=jnp.float32
            ) * (inverse * scale)
            primal = both[:, :HD]
            res[h, 0, mine, :] = primal.astype(jnp.bfloat16)
            res[h, 1, mine, :] = (along + both[:, HD:] - correction * primal).astype(jnp.bfloat16)

            @pl.when(h == heads - 1)
            def _():
                for k in range(per):
                    for i in range(2):
                        send_out(i, at * per + k, h)

        @pl.when(h < heads - 1)
        def _():
            @pl.loop(0, n // turns)
            def _(step):
                for i in range(2):
                    for turn in range(turns):
                        send_out(i, alternating(me, step * turns + turn, n), h)

    @pl.loop(0, heads)
    def _(h):
        wait_bytes(big.at[h, :, pl.ds(0, rest), :], send_sem.at[h])
        wait_bytes(res.at[h, :, pl.ds(0, rest), :], osend_sem.at[h])
        for i in range(2):
            own_out(i, h).wait()

    wait_bytes(res.at[:, :, pl.ds(0, rest), :], orecv_sem)


def body(*arrays):
    n = lax.axis_size("ctx")
    rows, width = arrays[0].shape
    heads = width // (n * HD)
    total = n * rows
    per = 2 if n % 2 == 0 and total <= 2048 else 1
    shape = jax.ShapeDtypeStruct((rows, width), jnp.bfloat16)
    anywhere = pl.BlockSpec(memory_space=pl.ANY)
    return pl.pallas_call(
        functools.partial(kernel, n, heads, rows, per),
        out_shape=(shape, shape),
        in_specs=[anywhere] * ARRAYS,
        out_specs=(anywhere, anywhere),
        scratch_shapes=[
            pltpu.VMEM((heads, 3, total, 2 * HD), jnp.bfloat16),
            pltpu.VMEM((heads, 2, total, HD), jnp.bfloat16),
            pltpu.SemaphoreType.DMA((heads,)),
            pltpu.SemaphoreType.DMA((heads,)),
            pltpu.SemaphoreType.DMA((heads, ARRAYS)),
            pltpu.SemaphoreType.DMA((heads,)),
            pltpu.SemaphoreType.DMA,
            pltpu.SemaphoreType.DMA((heads, 2)),
        ],
        compiler_params=pltpu.CompilerParams(
            collective_id=0, has_side_effects=True, vmem_limit_bytes=51 * 2**20
        ),
        cost_estimate=pl.CostEstimate(
            flops=12 * heads * total * total * HD,
            bytes_accessed=2 * 8 * rows * width,
            transcendentals=heads * total * total,
        ),
    )(*arrays)


def solution(mesh):
    spec = P(("clip", "ctx"), None)
    return jax.shard_map(
        body, mesh=mesh, in_specs=(spec,) * ARRAYS, out_specs=(spec, spec), check_vma=False
    )
```
